32 devices in a mesh: groups: 2 (over x), node: 16 (over z, y, core).
Axes of the slice: x: 2, y: 2, z: 4, core: 2. Of those that a mesh axis runs over, the one named last changes fastest.
Arguments:
- tokens: bfloat16 [4096, 4096], P(('groups', 'node')), parts along dimension 0, may hold values from -6 to 6
- steer_table: bfloat16 [256, 4096], P(('groups', 'node')), parts along dimension 0, may hold values from -6 to 6
- steer_index: int32 [4096], P(('groups', 'node')), parts along dimension 0, may hold values from 0 to 127
- sweep_coef: float32 [4096], P(('groups', 'node')), parts along dimension 0, may hold values from -3 to 3
- expert_ids: int32 [4096, 4], P(('groups', 'node')), parts along dimension 0, may hold values from 0 to 7, all different within a row; in each aligned block of 128 rows (0 to 127, 128 to 255, ...) at most 80 rows name the same one
- gate_level: int32 [4096, 4], P(('groups', 'node')), parts along dimension 0, may hold values from 0 to 15
- w_gate: bfloat16 [16, 4096, 768], P('node'), may hold values from -0.09375 to 0.09375
- w_up: bfloat16 [16, 4096, 768], P('node'), may hold values from -0.09375 to 0.09375
- w_down: bfloat16 [16, 768, 4096], P('node'), may hold values from -0.15625 to 0.15625
Outputs:
- mixed: bfloat16 [4096, 4096], P(('groups', 'node')), parts along dimension 0
The draws below stay inside these ranges and needn't reach their ends.
There are 2 independent parts, one for each index of `groups`. The reference program is written for one: setup_inputs(seed, part) draws one part's arguments, and reference() takes and returns one part's arrays. A program takes and returns all parts, laid end to end along the dimension named above; an argument that names none is the same for every part. Nothing has to cross between parts.
Inputs may be any that keep to these rules, and one draw needn't show every extreme that they name: `expert_ids`: each row names 4 different experts. Among the rows of one device no expert is named more than 80 times, a bound that some block reaches.
All inputs are finite; a program needn't handle non-finite values.
Results may differ from the reference program's by a relative error of at most 0.0085.
Values may be sent and summed in bfloat16 or wider, within the bound.
A program may use at most 128 MiB of HBM per device.

```python
import math
import jax
import jax.numpy as jnp
import numpy as np
from jax import lax

D = 4096
FF = 1536
FFH = 768
TOK_DEV = 128
TOKENS = 2048
EXPERTS = 8
HALVES = 16
TOP = 4
CAP = 80
NSTEER = 128
N_NODE = 16


def set_ends(result, key, smallest, largest):
    longest = result.shape.index(max(result.shape))
    spots = []
    for shift in (0, 1):
        where = [jax.random.randint(jax.random.fold_in(key, axis), (), 0, length) for axis, length in enumerate(result.shape)]
        where[longest] = (where[longest] + shift) % result.shape[longest]
        spots.append(tuple(where))
    return result.at[spots[0]].set(smallest).at[spots[1]].set(largest)


def steps_of(stream_key, extent, pieces, least, high):
    def one(dim, blocks):
        steps = jax.random.uniform(jax.random.fold_in(jax.random.fold_in(stream_key, 6), dim), (blocks,), jnp.float32, least / len(pieces), high / len(pieces))
        return jnp.repeat(jnp.exp(steps), extent[dim] // blocks).reshape((-1,) + (1,) * (len(extent) - dim - 1))

    factor_of = one(*pieces[0])
    for cut in pieces[1:]:
        factor_of = factor_of * one(*cut)
    return factor_of


def assign_block(stream_key, own, number, rows, count, top, limit, skew):
    sequence = jax.random.permutation(stream_key, count)
    packed, common = load_shares(count, rows * top, limit, skew, True), load_shares(count, rows * top, limit, skew, False)
    places = jnp.arange(count)

    def named(sizes, rotation):
        used = int((sizes > 0).sum())
        fixed = max(1, used // 4)
        moved = fixed + (places - fixed + rotation * (used - fixed)) % max(1, count - fixed)
        return jnp.zeros((count,), jnp.int32).at[sequence[jnp.where(places < fixed, places, moved)]].set(jnp.asarray(sizes, jnp.int32))

    sizes = jnp.where(number % 4 == 0, named(packed, number // 4), named(common, number - number // 4 - 1))
    mixed = jax.random.permutation(jax.random.fold_in(own, 3), count)
    donor, taker = mixed[0:count // 2 * 2:2], mixed[1:count // 2 * 2:2]
    slack = jnp.minimum(sizes[donor] - 1, limit - sizes[taker]) // 2
    slack = jnp.where((donor == sequence[0]) | (taker == sequence[0]) | (sizes[taker] == 0), 0, jnp.maximum(slack, 0))
    moved = jax.random.randint(jax.random.fold_in(own, 4), (count // 2,), 0, 1 << 20) % (slack + 1)
    sizes = sizes.at[donor].add(-moved).at[taker].add(moved)
    members = jnp.searchsorted(jnp.cumsum(sizes), jnp.arange(rows * top), side="right").astype(jnp.int32)
    listing = members.reshape(top, rows).T
    listing = listing[jax.random.permutation(jax.random.fold_in(own, 1), rows)]
    rotation = jax.random.randint(jax.random.fold_in(own, 2), (rows, 1), 0, top)
    return jnp.take_along_axis(listing, (jnp.arange(top)[None, :] + rotation) % top, axis=1)


def load_shares(count, total, limit, lean, full):
    portions = [(1 << 20) // math.isqrt(rank ** lean) + 1 for rank in range(1, count + 1)]
    largest = limit if full else min(limit, max(-(-total // count), total * portions[0] // sum(portions)))
    least = 1 if total - largest >= count - 1 else 0
    counts, rest = [largest] + [least] * (count - 1), total - largest - least * (count - 1)
    while rest > 0:
        free = [i for i in range(1, count) if counts[i] < largest] or [i for i in range(1, count) if counts[i] < limit]
        mass, remaining = sum([portions[i] for i in free]), rest
        for i in free:
            addition = min(limit - counts[i], max(1, remaining * portions[i] // mass), rest)
            counts[i] = counts[i] + addition
            rest = rest - addition
    return np.array(counts)


def noise(rng, extent, deviation, limit, cuts=(), kind=jnp.bfloat16):
    factor_of = steps_of(rng, extent, cuts, -0.22, 0.18) if cuts else 1.0
    entries = jax.random.normal(rng, extent, jnp.float32) * deviation * factor_of
    return jnp.minimum(jnp.maximum(entries, -limit), limit).astype(kind)


def setup_inputs(seed: int = 0, part: int = 0) -> dict:
    key_list = jax.random.split(jax.random.key(seed), 10)
    part_keys = jax.random.split(jax.random.fold_in(key_list[9], part), 10)
    tokens = noise(part_keys[0], (TOKENS, D), 1.0, 6.0, ((0, 16),))
    steer_table = noise(part_keys[1], (NSTEER, D), 1.0, 6.0, ((0, 16),))
    steer_index = set_ends(jax.random.randint(part_keys[2], (TOKENS,), 0, NSTEER), jax.random.fold_in(part_keys[2], 1), 0, NSTEER - 1).astype(jnp.int32)
    sweep_coef = jnp.clip(jax.random.uniform(part_keys[3], (TOKENS,), jnp.float32, -3.0, 3.0) * steps_of(part_keys[3], (TOKENS,), ((0, 16),), -0.4, 0.0), -3.0, 3.0)
    expert_ids_keys = jax.random.split(jax.random.fold_in(part_keys[4], 1), TOKENS // TOK_DEV)
    expert_ids_turns = jax.random.permutation(jax.random.fold_in(part_keys[4], 3), TOKENS // TOK_DEV)
    expert_ids = jax.vmap(lambda own, number: assign_block(jax.random.fold_in(part_keys[4], 2), own, number, TOK_DEV, EXPERTS, TOP, CAP, 2))(expert_ids_keys, expert_ids_turns).reshape((TOKENS, TOP))
    gate_level = set_ends(jax.random.randint(part_keys[5], (TOKENS, TOP), 0, 16), jax.random.fold_in(part_keys[5], 1), 0, 15).astype(jnp.int32)
    w_gate = noise(key_list[6], (HALVES, D, FFH), D ** -0.5, 0.09375, ((0, 16),))
    w_up = noise(key_list[7], (HALVES, D, FFH), D ** -0.5, 0.09375, ((0, 16),))
    w_down = noise(key_list[8], (HALVES, FFH, D), FF ** -0.5, 0.15625, ((0, 16),))
    return dict(tokens=tokens, steer_table=steer_table, steer_index=steer_index, sweep_coef=sweep_coef, expert_ids=expert_ids, gate_level=gate_level, w_gate=w_gate, w_up=w_up, w_down=w_down)


def reference(tokens, steer_table, steer_index, sweep_coef, expert_ids, gate_level, w_gate, w_up, w_down):
    steer = steer_table[steer_index].astype(jnp.float32)
    steered = tokens.astype(jnp.float32) + sweep_coef[:, None] * steer
    scale = lax.rsqrt(lax.optimization_barrier(jnp.mean(steered * steered, axis=1, keepdims=True)) + 1e-06)
    normed = (steered * scale).astype(jnp.bfloat16)
    levels = (gate_level + 1).astype(jnp.float32)
    share = levels / lax.optimization_barrier(jnp.sum(levels, axis=1, keepdims=True))
    capacity = N_NODE * CAP

    def half_output(rows, half_index):
        gate_part = lax.dynamic_index_in_dim(w_gate, half_index, 0, False)
        up_part = lax.dynamic_index_in_dim(w_up, half_index, 0, False)
        down_part = lax.dynamic_index_in_dim(w_down, half_index, 0, False)
        gate = jnp.dot(rows, gate_part, preferred_element_type=jnp.float32)
        upper = jnp.dot(rows, up_part, preferred_element_type=jnp.float32)
        act = (jax.nn.silu(gate) * upper).astype(jnp.bfloat16)
        return jnp.dot(act, down_part, preferred_element_type=jnp.float32).astype(jnp.bfloat16)

    def one_expert(total, expert):
        hit = expert_ids == expert
        row_weight = lax.optimization_barrier(jnp.sum(jnp.where(hit, share, 0.0), axis=1))
        routed = jnp.any(hit, axis=1)
        picked = jnp.nonzero(routed, size=capacity, fill_value=0)[0].astype(jnp.int32)
        count = jnp.sum(routed.astype(jnp.int32))
        valid = jnp.arange(capacity, dtype=jnp.int32) < count
        rows = normed[picked]
        first = half_output(rows, 2 * expert)
        second = half_output(rows, 2 * expert + 1)
        pair = (first.astype(jnp.float32) + second.astype(jnp.float32)).astype(jnp.bfloat16)
        pair = lax.optimization_barrier(pair).astype(jnp.float32)
        weight = jnp.where(valid, row_weight[picked], 0.0)
        return (total.at[picked].add(pair * weight[:, None]), None)
    start = jnp.zeros((TOKENS, D), jnp.float32)
    total, _ = lax.scan(one_expert, start, jnp.arange(EXPERTS, dtype=jnp.int32))
    return total.astype(jnp.bfloat16)
```

```python
import functools
import jax
import jax.numpy as jnp
from jax import lax
from jax.experimental import pallas as pl
from jax.experimental.pallas import tpu as pltpu
from jax.sharding import PartitionSpec as P


def on_device_any(
    tokens, steer_table, steer_index, sweep_coef, expert_ids, gate_level, w_gate, w_up, w_down
):
    tok_rows, width = tokens.shape
    top_count = expert_ids.shape[1]
    nodes = lax.axis_size("node")
    experts = nodes // 2
    slots = 2 * ((tok_rows * top_count * 5 + 8 * experts - 1) // (8 * experts))
    piece = lax.all_gather(steer_table, "node", axis=0, tiled=True)
    columns = lax.iota(jnp.int32, piece.shape[0])
    picker = (steer_index[:, None] == columns[None, :]).astype(jnp.bfloat16)
    steer = jnp.dot(picker, piece, preferred_element_type=jnp.float32)
    steered = tokens.astype(jnp.float32) + sweep_coef[:, None] * steer
    scale = lax.rsqrt(jnp.mean(steered * steered, axis=1, keepdims=True) + 1e-06)
    normed = (steered * scale).astype(jnp.bfloat16)
    flat_ids = expert_ids.reshape(-1)
    onehot = (flat_ids[:, None] == lax.iota(jnp.int32, experts)[None, :]).astype(jnp.int32)
    rank = jnp.cumsum(onehot, axis=0) - onehot
    slot_of = jnp.sum(onehot * rank, axis=1)
    target = (flat_ids * slots + slot_of).reshape(tok_rows, top_count)
    places = lax.iota(jnp.int32, experts * slots)
    matched = target[:, :, None] == places[None, None, :]
    select = jnp.any(matched, axis=1).astype(jnp.bfloat16)
    levels = (gate_level + 1).astype(jnp.float32)
    share = levels / jnp.sum(levels, axis=1, keepdims=True)
    mixing = jnp.sum(jnp.where(matched, share[:, :, None], 0.0), axis=1)
    packed = jnp.einsum("tr,td->rd", select, normed, preferred_element_type=jnp.float32).astype(
        jnp.bfloat16
    )
    doubled = jnp.broadcast_to(packed.reshape(experts, 1, slots, width), (experts, 2, slots, width))
    doubled = doubled.reshape(nodes, slots, width)
    block = lax.all_to_all(doubled, "node", split_axis=0, concat_axis=0, tiled=True)
    rows = block.reshape(-1, width)
    gate = jnp.dot(rows, w_gate[0], preferred_element_type=jnp.float32)
    upper = jnp.dot(rows, w_up[0], preferred_element_type=jnp.float32)
    act = (jax.nn.silu(gate) * upper).astype(jnp.bfloat16)
    partial_value = (
        jnp.dot(act, w_down[0], preferred_element_type=jnp.float32)
        .astype(jnp.bfloat16)
        .reshape(block.shape)
    )
    back = lax.all_to_all(partial_value, "node", split_axis=0, concat_axis=0, tiled=True).reshape(
        experts, 2, slots, width
    )
    summed = back[:, 0].astype(jnp.float32) + back[:, 1].astype(jnp.float32)
    total = summed.astype(jnp.bfloat16).reshape(experts * slots, width)
    mix_high = mixing.astype(jnp.bfloat16)
    mix_low = (mixing - mix_high.astype(jnp.float32)).astype(jnp.bfloat16)
    mixed = jnp.dot(mix_high, total, preferred_element_type=jnp.float32)
    mixed = mixed + jnp.dot(mix_low, total, preferred_element_type=jnp.float32)
    return mixed.astype(jnp.bfloat16)


CHIPS = 8
MIB = 1 << 20


def node_of(position, core):
    side = lax.div(position, 4)
    level = position + side * (7 - 2 * position)
    return (2 * level + side) * 2 + core


def position_of(chip):
    side, level = lax.rem(chip, 2), lax.div(chip, 2)
    return level + side * (7 - 2 * level)


def ring_kernel(
    tokens, shard, meta, gate_hbm, up_hbm, down_hbm, out,
    tok, both, sums, table, metas, steered, act, w_gate, w_up, w_down,
    w_sem, ag_send, ag_recv, meta_send, meta_recv, tab_send, tab_recv,
    norm_send, norm_recv, part_send, part_recv, rs_send, rs_recv, free_sem,
):
    rows, width = tokens.shape
    half = rows // 2
    hidden = w_gate.shape[1]
    node = lax.axis_index("node")
    chip, core = lax.div(node, 2), lax.rem(node, 2)
    here = position_of(chip)

    def ring(distance):
        return {"node": node_of(lax.rem(here + distance + CHIPS, CHIPS), core)}

    sibling = {"node": 2 * chip + 1 - core}
    right, left = ring(1), ring(-1)
    mine = pl.ds(pl.multiple_of(core * rows, rows), rows)
    others = pl.ds(pl.multiple_of((1 - core) * rows, rows), rows)

    loads = [
        pltpu.make_async_copy(src, dst, w_sem.at[i])
        for i, (src, dst) in enumerate(((gate_hbm.at[0], w_gate), (up_hbm.at[0], w_up), (down_hbm.at[0], w_down)))
    ]
    for load in loads:
        load.start()

    barrier = pltpu.get_barrier_semaphore()
    for distance in range(1, CHIPS):
        pl.semaphore_signal(barrier, inc=1, device_id=ring(distance), device_id_type=pl.DeviceIdType.MESH)
    pl.semaphore_signal(barrier, inc=1, device_id=sibling, device_id_type=pl.DeviceIdType.MESH)
    pl.semaphore_wait(barrier, CHIPS)

    def send(src, dst, send_sem, recv_sem, device):
        copy = pltpu.make_async_remote_copy(
            src_ref=src, dst_ref=dst, send_sem=send_sem, recv_sem=recv_sem,
            device_id=device, device_id_type=pl.DeviceIdType.MESH,
        )
        copy.start()
        return copy

    shard_rows = shard.shape[0]
    my_shard = pl.ds(pl.multiple_of((core * CHIPS + here) * shard_rows, shard_rows), shard_rows)
    side_rows = CHIPS * shard_rows
    my_side = pl.ds(pl.multiple_of(core * side_rows, side_rows), side_rows)
    meta_copies, tab_copies = {}, {}
    for distance in range(1, CHIPS):
        slot = CHIPS - distance
        tab_copies[slot] = send(shard, table.at[my_shard], tab_send.at[slot], tab_recv.at[slot], ring(distance))
        meta_copies[slot] = send(meta, metas.at[slot], meta_send.at[slot], meta_recv.at[slot], ring(distance))

    ag = {}
    ag[1] = send(tokens, tok.at[1], ag_send.at[1], ag_recv.at[1], left)
    ag[7] = send(tokens, tok.at[7], ag_send.at[7], ag_recv.at[7], right)

    metas[0] = meta[...]
    table[my_shard, :] = shard[...]
    sums[3, half:, :] = jnp.zeros((half, width), jnp.bfloat16)
    sums[5, :half, :] = jnp.zeros((half, width), jnp.bfloat16)
    for slot in range(1, CHIPS):
        tab_copies[slot].wait_recv()
        meta_copies[slot].wait_recv()
    side_copy = send(table.at[my_side], table.at[my_side], tab_send.at[0], tab_recv.at[0], sibling)
    side_copy.wait_recv()

    def columns_of(slot):
        wide = jnp.concatenate([metas[slot], jnp.zeros((128 - meta.shape[0], rows), jnp.float32)], axis=0)
        return jnp.transpose(wide)

    def pick(columns, which):
        lanes = lax.broadcasted_iota(jnp.int32, columns.shape, 1)
        return jnp.sum(jnp.where(lanes == which, columns, 0.0), axis=1, keepdims=True)

    def norm(slot):
        columns = columns_of(slot)
        coef, place = pick(columns, CHIPS), pick(columns, CHIPS + 1)
        lanes = lax.broadcasted_iota(jnp.int32, (rows, table.shape[0]), 1).astype(jnp.float32)
        tile = 512
        side_width = table.shape[1]
        total = jnp.zeros((rows, 1), jnp.float32)
        for side in range(2):
            picker = (lanes == place + side).astype(jnp.bfloat16)

            def body(j, total):
                narrow = pl.ds(pl.multiple_of(j * tile, tile), tile)
                cols = pl.ds(pl.multiple_of(side * side_width + j * tile, tile), tile)
                source = tokens[:, cols] if slot == 0 else tok[slot, :, cols]
                steer = jnp.dot(picker, table[:, narrow], preferred_element_type=jnp.float32)
                value = source.astype(jnp.float32) + coef * steer
                steered[:, cols] = value
                return total + jnp.sum(value * value, axis=1, keepdims=True)

            total = lax.fori_loop(0, side_width // tile, body, total)
        scale = lax.rsqrt(total * (1.0 / width) + 1e-06)

        @pl.loop(0, width // tile)
        def _(j):
            cols = pl.ds(pl.multiple_of(j * tile, tile), tile)
            both[slot, mine, cols] = (steered[:, cols] * scale).astype(jnp.bfloat16)

        return send(
            both.at[slot, mine], both.at[slot, mine], norm_send.at[slot], norm_recv.at[slot], sibling
        )

    def feed_forward(slot):
        tile = 256

        @pl.loop(0, hidden // tile)
        def _(j):
            cols = pl.ds(pl.multiple_of(j * tile, tile), tile)
            gate = jnp.dot(both[slot], w_gate[:, cols], preferred_element_type=jnp.float32)
            upper = jnp.dot(both[slot], w_up[:, cols], preferred_element_type=jnp.float32)
            act[:, cols] = (gate / (1.0 + jnp.exp(-gate)) * upper).astype(jnp.bfloat16)

        tile = 512

        @pl.loop(0, width // tile)
        def _(j):
            cols = pl.ds(pl.multiple_of(j * tile, tile), tile)
            both[slot, :, cols] = jnp.dot(
                act[...], w_down[:, cols], preferred_element_type=jnp.float32
            ).astype(jnp.bfloat16)

    def send_partial(slot):
        return send(both.at[slot, others], tok.at[slot], part_send.at[slot], part_recv.at[slot], sibling)

    def tell_free(slot):
        pl.semaphore_signal(free_sem.at[slot], inc=1, device_id=sibling, device_id_type=pl.DeviceIdType.MESH)

    norms, parts = {}, {}
    norms[0] = norm(0)
    for load in loads:
        load.wait()
    norms[0].wait()
    feed_forward(0)
    parts[0] = send_partial(0)

    def release(slots):
        for slot in slots:
            ag_next[slot].wait_send()
            tell_free(slot)
        for slot in slots:
            pl.semaphore_wait(free_sem.at[slot], 1)
            parts[slot] = send_partial(slot)

    ag_next = {}
    for step in (1, 2, 3):
        up, down = step, CHIPS - step
        ag[up].wait_recv()
        if step < 3:
            ag[up + 1] = ag_next[up] = send(
                tok.at[up], tok.at[up + 1], ag_send.at[up + 1], ag_recv.at[up + 1], left
            )
        else:
            first = ag_next[up] = send(
                tok.at[up, pl.ds(0, half)], tok.at[4, pl.ds(0, half)], ag_send.at[4], ag_recv.at[4], left
            )
        ag[down].wait_recv()
        if step < 3:
            ag[down - 1] = ag_next[down] = send(
                tok.at[down], tok.at[down - 1], ag_send.at[down - 1], ag_recv.at[down - 1], right
            )
        else:
            second = ag_next[down] = send(
                tok.at[down, pl.ds(half, half)], tok.at[4, pl.ds(half, half)], ag_send.at[0], ag_recv.at[0], right
            )
        for slot in (up, down):
            norms[slot] = norm(slot)
        for slot in (up, down):
            norms[slot].wait()
            feed_forward(slot)
        if step > 1:
            release((step - 1, CHIPS - step + 1))
    first.wait_recv()
    second.wait_recv()
    norms[4] = norm(4)
    tell_free(4)
    norms[4].wait()
    feed_forward(4)
    pl.semaphore_wait(free_sem.at[4], 1)
    parts[4] = send_partial(4)
    release((3, 5))

    def combine(slot, incoming, target):
        parts[slot].wait_recv()
        weight = pick(columns_of(slot), chip)
        tile = 512

        @pl.loop(0, width // tile)
        def _(j):
            cols = pl.ds(pl.multiple_of(j * tile, tile), tile)
            pair = both[slot, mine, cols].astype(jnp.float32) + tok[slot, :, cols].astype(jnp.float32)
            value = weight * pair.astype(jnp.bfloat16).astype(jnp.float32)
            for index in incoming:
                value = value + sums[index, :, cols].astype(jnp.float32)
            if target is None:
                both[slot, mine, cols] = value.astype(jnp.bfloat16)
            else:
                target[:, cols] = value.astype(jnp.bfloat16)

    combine(4, (), None)
    low = pl.ds(pl.multiple_of(core * rows, half), half)
    high = pl.ds(pl.multiple_of(core * rows + half, half), half)
    rs = {}
    rs[3] = send(both.at[4, low], sums.at[3, pl.ds(0, half)], rs_send.at[3], rs_recv.at[3], right)
    rs[5] = send(both.at[4, high], sums.at[5, pl.ds(half, half)], rs_send.at[5], rs_recv.at[5], left)
    for step in (3, 2, 1):
        up, down = step, CHIPS - step
        rs[up].wait_recv()
        combine(up, (up,), None)
        after = up - 1
        rs[after] = send(both.at[up, mine], sums.at[after], rs_send.at[after], rs_recv.at[after], right)
        rs[down].wait_recv()
        combine(down, (down,), None)
        after = down + 1 if down < 7 else 4
        rs[after] = send(both.at[down, mine], sums.at[after], rs_send.at[after], rs_recv.at[after], left)
    rs[0].wait_recv()
    rs[4].wait_recv()
    combine(0, (0, 4), out)

    for slot in range(CHIPS):
        rs[slot].wait_send()
        parts[slot].wait_send()
    ag[1].wait_send()
    ag[7].wait_send()
    side_copy.wait_send()
    for slot in range(1, CHIPS):
        tab_copies[slot].wait_send()
        meta_copies[slot].wait_send()


def on_device_ring(
    tokens, steer_table, steer_index, sweep_coef, expert_ids, gate_level, w_gate, w_up, w_down
):
    rows, width = tokens.shape
    hidden = w_gate.shape[2]
    per_device = steer_table.shape[0]
    levels = (gate_level + 1).astype(jnp.float32)
    share = levels / jnp.sum(levels, axis=1, keepdims=True)
    hit = expert_ids.T[None, :, :] == lax.iota(jnp.int32, CHIPS)[:, None, None]
    mixing = jnp.sum(jnp.where(hit, share.T[None, :, :], 0.0), axis=1)
    owner = steer_index // per_device
    slot = (owner % 2) * CHIPS + position_of(owner // 2)
    place = 2 * (slot * per_device + steer_index % per_device)
    meta = jnp.concatenate(
        [
            mixing,
            sweep_coef[None, :],
            place.astype(jnp.float32)[None, :],
            jnp.zeros((16 - CHIPS - 2, rows), jnp.float32),
        ],
        axis=0,
    )
    shard = steer_table.reshape(2 * per_device, width // 2)
    vmem = pl.BlockSpec(memory_space=pltpu.VMEM)
    hbm = pl.BlockSpec(memory_space=pl.ANY)
    dma = pltpu.SemaphoreType.DMA
    return pl.pallas_call(
        ring_kernel,
        out_shape=jax.ShapeDtypeStruct((rows, width), jnp.bfloat16),
        in_specs=[vmem, vmem, vmem, hbm, hbm, hbm],
        out_specs=vmem,
        scratch_shapes=[
            pltpu.VMEM((CHIPS, rows, width), jnp.bfloat16),
            pltpu.VMEM((CHIPS, 2 * rows, width), jnp.bfloat16),
            pltpu.VMEM((CHIPS, rows, width), jnp.bfloat16),
            pltpu.VMEM((2 * CHIPS * 2 * per_device, width // 2), jnp.bfloat16),
            pltpu.VMEM((CHIPS, 16, rows), jnp.float32),
            pltpu.VMEM((rows, width), jnp.float32),
            pltpu.VMEM((2 * rows, hidden), jnp.bfloat16),
            pltpu.VMEM((width, hidden), jnp.bfloat16),
            pltpu.VMEM((width, hidden), jnp.bfloat16),
            pltpu.VMEM((hidden, width), jnp.bfloat16),
            dma((3,)),
        ]
        + [dma((CHIPS,)) for _ in range(12)]
        + [pltpu.SemaphoreType.REGULAR((CHIPS,))],
        compiler_params=pltpu.CompilerParams(
            collective_id=0, has_side_effects=True, vmem_limit_bytes=62 * MIB
        ),
    )(tokens, shard, meta, w_gate, w_up, w_down)


def solution(mesh):
    return jax.shard_map(
        on_device_ring if mesh.shape["node"] == 16 else on_device_any,
        mesh=mesh,
        in_specs=(
            P(("groups", "node"), None),
            P(("groups", "node"), None),
            P(("groups", "node")),
            P(("groups", "node")),
            P(("groups", "node"), None),
            P(("groups", "node"), None),
            P("node", None, None),
            P("node", None, None),
            P("node", None, None),
        ),
        out_specs=P(("groups", "node"), None),
        check_vma=False,
    )
```

```python
import functools
import jax
import jax.numpy as jnp
from jax import lax
from jax.experimental import pallas as pl
from jax.experimental.pallas import tpu as pltpu
from jax.sharding import PartitionSpec as P


def on_device_any(
    tokens, steer_table, steer_index, sweep_coef, expert_ids, gate_level, w_gate, w_up, w_down
):
    tok_rows, width = tokens.shape
    top_count = expert_ids.shape[1]
    nodes = lax.axis_size("node")
    experts = nodes // 2
    slots = 2 * ((tok_rows * top_count * 5 + 8 * experts - 1) // (8 * experts))
    piece = lax.all_gather(steer_table, "node", axis=0, tiled=True)
    columns = lax.iota(jnp.int32, piece.shape[0])
    picker = (steer_index[:, None] == columns[None, :]).astype(jnp.bfloat16)
    steer = jnp.dot(picker, piece, preferred_element_type=jnp.float32)
    steered = tokens.astype(jnp.float32) + sweep_coef[:, None] * steer
    scale = lax.rsqrt(jnp.mean(steered * steered, axis=1, keepdims=True) + 1e-06)
    normed = (steered * scale).astype(jnp.bfloat16)
    flat_ids = expert_ids.reshape(-1)
    onehot = (flat_ids[:, None] == lax.iota(jnp.int32, experts)[None, :]).astype(jnp.int32)
    rank = jnp.cumsum(onehot, axis=0) - onehot
    slot_of = jnp.sum(onehot * rank, axis=1)
    target = (flat_ids * slots + slot_of).reshape(tok_rows, top_count)
    places = lax.iota(jnp.int32, experts * slots)
    matched = target[:, :, None] == places[None, None, :]
    select = jnp.any(matched, axis=1).astype(jnp.bfloat16)
    levels = (gate_level + 1).astype(jnp.float32)
    share = levels / jnp.sum(levels, axis=1, keepdims=True)
    mixing = jnp.sum(jnp.where(matched, share[:, :, None], 0.0), axis=1)
    packed = jnp.einsum("tr,td->rd", select, normed, preferred_element_type=jnp.float32).astype(
        jnp.bfloat16
    )
    doubled = jnp.broadcast_to(packed.reshape(experts, 1, slots, width), (experts, 2, slots, width))
    doubled = doubled.reshape(nodes, slots, width)
    block = lax.all_to_all(doubled, "node", split_axis=0, concat_axis=0, tiled=True)
    rows = block.reshape(-1, width)
    gate = jnp.dot(rows, w_gate[0], preferred_element_type=jnp.float32)
    upper = jnp.dot(rows, w_up[0], preferred_element_type=jnp.float32)
    act = (jax.nn.silu(gate) * upper).astype(jnp.bfloat16)
    partial_value = (
        jnp.dot(act, w_down[0], preferred_element_type=jnp.float32)
        .astype(jnp.bfloat16)
        .reshape(block.shape)
    )
    back = lax.all_to_all(partial_value, "node", split_axis=0, concat_axis=0, tiled=True).reshape(
        experts, 2, slots, width
    )
    summed = back[:, 0].astype(jnp.float32) + back[:, 1].astype(jnp.float32)
    total = summed.astype(jnp.bfloat16).reshape(experts * slots, width)
    mix_high = mixing.astype(jnp.bfloat16)
    mix_low = (mixing - mix_high.astype(jnp.float32)).astype(jnp.bfloat16)
    mixed = jnp.dot(mix_high, total, preferred_element_type=jnp.float32)
    mixed = mixed + jnp.dot(mix_low, total, preferred_element_type=jnp.float32)
    return mixed.astype(jnp.bfloat16)


CHIPS = 8
PARTS = 2
MIB = 1 << 20


def node_of(position, core):
    side = lax.div(position, 4)
    level = position + side * (7 - 2 * position)
    return (2 * level + side) * 2 + core


def position_of(chip):
    side, level = lax.rem(chip, 2), lax.div(chip, 2)
    return level + side * (7 - 2 * level)


def ring_kernel(
    tokens, shard, meta, gate_hbm, up_hbm, down_hbm, out,
    tok, both, sums, table, metas, steered, act, w_gate, w_up, w_down,
    w_sem, ag_send, ag_recv, meta_send, meta_recv, tab_send, tab_recv,
    norm_send, norm_recv, part_send, part_recv, rs_send, rs_recv, free_sem,
):
    rows, width = tokens.shape
    size = rows // PARTS
    half = size // 2
    hidden = w_gate.shape[1]
    node = lax.axis_index("node")
    chip, core = lax.div(node, 2), lax.rem(node, 2)
    here = position_of(chip)

    def ring(distance):
        return {"node": node_of(lax.rem(here + distance + CHIPS, CHIPS), core)}

    sibling = {"node": 2 * chip + 1 - core}
    right, left = ring(1), ring(-1)
    mine = pl.ds(pl.multiple_of(core * rows, rows), rows)
    others = pl.ds(pl.multiple_of((1 - core) * rows, rows), rows)

    loads = [
        pltpu.make_async_copy(src, dst, w_sem.at[i])
        for i, (src, dst) in enumerate(((gate_hbm.at[0], w_gate), (up_hbm.at[0], w_up), (down_hbm.at[0], w_down)))
    ]
    for load in loads:
        load.start()

    barrier = pltpu.get_barrier_semaphore()
    for distance in range(1, CHIPS):
        pl.semaphore_signal(barrier, inc=1, device_id=ring(distance), device_id_type=pl.DeviceIdType.MESH)
    pl.semaphore_signal(barrier, inc=1, device_id=sibling, device_id_type=pl.DeviceIdType.MESH)
    pl.semaphore_wait(barrier, CHIPS)

    def send(src, dst, send_sem, recv_sem, device):
        copy = pltpu.make_async_remote_copy(
            src_ref=src, dst_ref=dst, send_sem=send_sem, recv_sem=recv_sem,
            device_id=device, device_id_type=pl.DeviceIdType.MESH,
        )
        copy.start()
        return copy

    shard_rows = shard.shape[0]
    my_shard = pl.ds(pl.multiple_of((core * CHIPS + here) * shard_rows, shard_rows), shard_rows)
    side_rows = CHIPS * shard_rows
    my_side = pl.ds(pl.multiple_of(core * side_rows, side_rows), side_rows)
    meta_copies, tab_copies = {}, {}
    for distance in range(1, CHIPS):
        slot = CHIPS - distance
        tab_copies[slot] = send(shard, table.at[my_shard], tab_send.at[slot], tab_recv.at[slot], ring(distance))
        meta_copies[slot] = send(meta, metas.at[slot], meta_send.at[slot], meta_recv.at[slot], ring(distance))

    ag = {}
    for part in range(PARTS):
        block = tokens.at[pl.ds(part * size, size)]
        ag[part, 1] = send(block, tok.at[part, 1], ag_send.at[part, 1], ag_recv.at[part, 1], left)
        ag[part, 7] = send(block, tok.at[part, 7], ag_send.at[part, 7], ag_recv.at[part, 7], right)

    metas[0] = meta[...]
    table[my_shard, :] = shard[...]
    for part in range(PARTS):
        sums[part, 3, half:, :] = jnp.zeros((half, width), jnp.bfloat16)
        sums[part, 5, :half, :] = jnp.zeros((half, width), jnp.bfloat16)
    for slot in range(1, CHIPS):
        tab_copies[slot].wait_recv()
        meta_copies[slot].wait_recv()
    side_copy = send(table.at[my_side], table.at[my_side], tab_send.at[0], tab_recv.at[0], sibling)
    side_copy.wait_recv()

    def columns_of(part, slot):
        wide = jnp.concatenate([metas[slot], jnp.zeros((128 - meta.shape[0], rows), jnp.float32)], axis=0)
        return jnp.transpose(wide)[part * size:(part + 1) * size]

    def pick(columns, which):
        lanes = lax.broadcasted_iota(jnp.int32, columns.shape, 1)
        return jnp.sum(jnp.where(lanes == which, columns, 0.0), axis=1, keepdims=True)

    def place_of(slot):
        if 1 <= slot <= 4:
            return slot - 1, 0
        return (CHIPS - 1 - slot, 1) if slot else (3, 1)

    def rows_of(part, slot, side):
        group, way = place_of(slot)
        start = pl.multiple_of(way * 2 * size + side * size, size)
        return both.at[part, group, pl.ds(start, size)]

    def norm(part, slot):
        columns = columns_of(part, slot)
        coef, place = pick(columns, CHIPS), pick(columns, CHIPS + 1)
        lanes = lax.broadcasted_iota(jnp.int32, (size, table.shape[0]), 1).astype(jnp.float32)
        tile = 512
        side_width = table.shape[1]
        total = jnp.zeros((size, 1), jnp.float32)
        target = rows_of(part, slot, core)
        for side in range(2):
            picker = (lanes == place + side).astype(jnp.bfloat16)

            def body(j, total):
                narrow = pl.ds(pl.multiple_of(j * tile, tile), tile)
                cols = pl.ds(pl.multiple_of(side * side_width + j * tile, tile), tile)
                source = tok[part, slot, :, cols] if slot else tokens[pl.ds(part * size, size), cols]
                steer = jnp.dot(picker, table[:, narrow], preferred_element_type=jnp.float32)
                value = source.astype(jnp.float32) + coef * steer
                steered[:, cols] = value
                return total + jnp.sum(value * value, axis=1, keepdims=True)

            total = lax.fori_loop(0, side_width // tile, body, total)
        scale = lax.rsqrt(total * (1.0 / width) + 1e-06)

        @pl.loop(0, width // tile)
        def _(j):
            cols = pl.ds(pl.multiple_of(j * tile, tile), tile)
            target[:, cols] = (steered[:, cols] * scale).astype(jnp.bfloat16)

        norms[part, slot] = send(
            target, target, norm_send.at[part, slot], norm_recv.at[part, slot], sibling
        )

    def feed_forward(part, group):
        tile = 256

        @pl.loop(0, hidden // tile)
        def _(j):
            cols = pl.ds(pl.multiple_of(j * tile, tile), tile)
            gate = jnp.dot(both[part, group], w_gate[:, cols], preferred_element_type=jnp.float32)
            upper = jnp.dot(both[part, group], w_up[:, cols], preferred_element_type=jnp.float32)
            act[:, cols] = (gate / (1.0 + jnp.exp(-gate)) * upper).astype(jnp.bfloat16)

        tile = 512

        @pl.loop(0, width // tile)
        def _(j):
            cols = pl.ds(pl.multiple_of(j * tile, tile), tile)
            both[part, group, :, cols] = jnp.dot(
                act[...], w_down[:, cols], preferred_element_type=jnp.float32
            ).astype(jnp.bfloat16)

    def tell_free(part, slot):
        pl.semaphore_signal(
            free_sem.at[part, slot], inc=1, device_id=sibling, device_id_type=pl.DeviceIdType.MESH
        )

    def run_group(part, step):
        slots = (step, CHIPS - step) if step < 4 else (4, 0)
        for slot in slots:
            norms[part, slot].wait()
        feed_forward(part, step - 1)
        for slot in slots:
            if slot % 4:
                forwards[part, slot].wait_send()
                tell_free(part, slot)
        for slot in slots:
            if slot:
                pl.semaphore_wait(free_sem.at[part, slot], 1)
            parts[part, slot] = send(
                rows_of(part, slot, 1 - core), tok.at[part, slot],
                part_send.at[part, slot], part_recv.at[part, slot], sibling,
            )

    norms, parts, forwards = {}, {}, {}
    for part in range(PARTS):
        norm(part, 0)
    for load in loads:
        load.wait()
    waiting = None
    for step in (1, 2, 3, 4):
        for part in range(PARTS):
            if step < 4:
                for slot, after, device in ((step, step + 1, left), (CHIPS - step, CHIPS - step - 1, right)):
                    ag[part, slot].wait_recv()
                    if step < 3:
                        src, dst, index = tok.at[part, slot], tok.at[part, after], after
                    else:
                        piece = pl.ds(0 if device is left else half, half)
                        src, dst = tok.at[part, slot, piece], tok.at[part, 4, piece]
                        index = 4 if device is left else 0
                    forwards[part, slot] = send(
                        src, dst, ag_send.at[part, index], ag_recv.at[part, index], device
                    )
                    ag[part, index] = forwards[part, slot]
                norm(part, step)
                norm(part, CHIPS - step)
            else:
                ag[part, 4].wait_recv()
                ag[part, 0].wait_recv()
                norm(part, 4)
                tell_free(part, 4)
            if waiting is not None:
                run_group(*waiting)
            waiting = (part, step)

    def combine(part, slot, incoming, target):
        parts[part, slot].wait_recv()
        weight = pick(columns_of(part, slot), chip)
        own = rows_of(part, slot, core)
        tile = 512

        @pl.loop(0, width // tile)
        def _(j):
            cols = pl.ds(pl.multiple_of(j * tile, tile), tile)
            pair = own[:, cols].astype(jnp.float32) + tok[part, slot, :, cols].astype(jnp.float32)
            value = weight * pair.astype(jnp.bfloat16).astype(jnp.float32)
            for index in incoming:
                value = value + sums[part, index, :, cols].astype(jnp.float32)
            target[:, cols] = value.astype(jnp.bfloat16)

    rs = {}

    def far_sums(part):
        combine(part, 4, (), rows_of(part, 4, core))
        start = pl.multiple_of(core * size, size)
        low = both.at[part, 3, pl.ds(start, half)]
        high = both.at[part, 3, pl.ds(pl.multiple_of(start + half, half), half)]
        rs[part, 3] = send(
            low, sums.at[part, 3, pl.ds(0, half)], rs_send.at[part, 3], rs_recv.at[part, 3], right
        )
        rs[part, 5] = send(
            high, sums.at[part, 5, pl.ds(half, half)], rs_send.at[part, 5], rs_recv.at[part, 5], left
        )

    for part in range(PARTS - 1):
        far_sums(part)
    run_group(*waiting)
    far_sums(PARTS - 1)
    for step in (3, 2, 1):
        for part in range(PARTS):
            for slot, after, device in (
                (step, step - 1, right), (CHIPS - step, CHIPS - step + 1 if step > 1 else 4, left)
            ):
                rs[part, slot].wait_recv()
                own = rows_of(part, slot, core)
                combine(part, slot, (slot,), own)
                rs[part, after] = send(
                    own, sums.at[part, after], rs_send.at[part, after], rs_recv.at[part, after], device
                )
    for part in range(PARTS):
        rs[part, 0].wait_recv()
        rs[part, 4].wait_recv()
        combine(part, 0, (0, 4), out.at[pl.ds(part * size, size)])

    for part in range(PARTS):
        for slot in range(CHIPS):
            rs[part, slot].wait_send()
            parts[part, slot].wait_send()
        ag[part, 1].wait_send()
        ag[part, 7].wait_send()
    side_copy.wait_send()
    for slot in range(1, CHIPS):
        tab_copies[slot].wait_send()
        meta_copies[slot].wait_send()


def on_device_ring(
    tokens, steer_table, steer_index, sweep_coef, expert_ids, gate_level, w_gate, w_up, w_down
):
    rows, width = tokens.shape
    hidden = w_gate.shape[2]
    per_device = steer_table.shape[0]
    levels = (gate_level + 1).astype(jnp.float32)
    share = levels / jnp.sum(levels, axis=1, keepdims=True)
    hit = expert_ids.T[None, :, :] == lax.iota(jnp.int32, CHIPS)[:, None, None]
    mixing = jnp.sum(jnp.where(hit, share.T[None, :, :], 0.0), axis=1)
    owner = steer_index // per_device
    slot = (owner % 2) * CHIPS + position_of(owner // 2)
    place = 2 * (slot * per_device + steer_index % per_device)
    meta = jnp.concatenate(
        [
            mixing,
            sweep_coef[None, :],
            place.astype(jnp.float32)[None, :],
            jnp.zeros((16 - CHIPS - 2, rows), jnp.float32),
        ],
        axis=0,
    )
    shard = steer_table.reshape(2 * per_device, width // 2)
    vmem = pl.BlockSpec(memory_space=pltpu.VMEM)
    hbm = pl.BlockSpec(memory_space=pl.ANY)
    dma = pltpu.SemaphoreType.DMA
    return pl.pallas_call(
        ring_kernel,
        out_shape=jax.ShapeDtypeStruct((rows, width), jnp.bfloat16),
        in_specs=[vmem, vmem, vmem, hbm, hbm, hbm],
        out_specs=vmem,
        scratch_shapes=[
            pltpu.VMEM((PARTS, CHIPS, rows // PARTS, width), jnp.bfloat16),
            pltpu.VMEM((PARTS, CHIPS // 2, 4 * rows // PARTS, width), jnp.bfloat16),
            pltpu.VMEM((PARTS, CHIPS, rows // PARTS, width), jnp.bfloat16),
            pltpu.VMEM((2 * CHIPS * 2 * per_device, width // 2), jnp.bfloat16),
            pltpu.VMEM((CHIPS, 16, rows), jnp.float32),
            pltpu.VMEM((rows // PARTS, width), jnp.float32),
            pltpu.VMEM((2 * rows, hidden), jnp.bfloat16),
            pltpu.VMEM((width, hidden), jnp.bfloat16),
            pltpu.VMEM((width, hidden), jnp.bfloat16),
            pltpu.VMEM((hidden, width), jnp.bfloat16),
            dma((3,)),
        ]
        + [dma((PARTS, CHIPS)), dma((PARTS, CHIPS))]
        + [dma((CHIPS,)) for _ in range(4)]
        + [dma((PARTS, CHIPS)) for _ in range(6)]
        + [pltpu.SemaphoreType.REGULAR((PARTS, CHIPS))],
        compiler_params=pltpu.CompilerParams(
            collective_id=0, has_side_effects=True, vmem_limit_bytes=62 * MIB
        ),
    )(tokens, shard, meta, w_gate, w_up, w_down)


def solution(mesh):
    return jax.shard_map(
        on_device_ring if mesh.shape["node"] == 16 else on_device_any,
        mesh=mesh,
        in_specs=(
            P(("groups", "node"), None),
            P(("groups", "node"), None),
            P(("groups", "node")),
            P(("groups", "node")),
            P(("groups", "node"), None),
            P(("groups", "node"), None),
            P("node", None, None),
            P("node", None, None),
            P("node", None, None),
        ),
        out_specs=P(("groups", "node"), None),
        check_vma=False,
    )
```
